1024 devices in a mesh: section: 32 (over z_hi, y, core), expert: 32 (over z_lo, x).
Axes of the slice: x: 4, y: 4, z: 32 (z_hi: 4, z_lo: 8; z = z_hi * 8 + z_lo), core: 2. Of those that a mesh axis runs over, the one named last changes fastest.
Arguments:
- states: bfloat16 [32, 256, 3584], P('section', 'expert'), may hold values from -6 to 6
- norm_gain: float32 [32, 3584], P('section'), may hold values from 0.1 to 1.9
- router: bfloat16 [32, 3584, 4], P('section'), may hold values from -0.09375 to 0.09375
- w_gate: bfloat16 [32, 3584, 4096], P('section', None, 'expert'), may hold values from -0.09375 to 0.09375
- w_up: bfloat16 [32, 3584, 4096], P('section', None, 'expert'), may hold values from -0.09375 to 0.09375
- w_down: bfloat16 [32, 4096, 3584], P('section', 'expert'), may hold values from -0.1875 to 0.1875
- routes: int32 [2, 32, 256, 2], P(None, 'section', 'expert'), may hold values from 0 to 3, all different within a row; in each aligned block of 8 rows (0 to 7, 8 to 15, ..., all dimensions but the last counted through in order) at most 8 rows name the same one
Outputs:
- final_states: bfloat16 [32, 256, 3584], P('section', 'expert')
The draws below stay inside these ranges and needn't reach their ends.
Inputs may be any that keep to these rules, and one draw needn't show every extreme that they name: `routes`: each token names 2 different experts. Within one tick and one section, among the 8 tokens of one index of the expert axis, no expert is named by more than 8 tokens; in some such blocks one expert is named by exactly 8.
All inputs are finite; a program needn't handle non-finite values.
Results may differ from the reference program's by a relative error of at most 0.0064.
Values may be sent and summed in bfloat16 or wider, within the bound.
A program may use at most 32 MiB of HBM per device.

```python
import math
import jax
import jax.numpy as jnp
import numpy as np
from jax import lax

D = 3584
FF = 1024
EXPERTS = 4
TOPK = 2
TICKS = 2
TOK_DEV = 8
SHARDS = 8
HID_DEV = 128
CAP = 8
SECTIONS = 32
TOKS = 256
N_EXPERT = 32


def levels(stream_key, extent, cuts, least, high):
    level = 1.0
    for dim, blocks in cuts:
        heights = jax.random.uniform(jax.random.fold_in(jax.random.fold_in(stream_key, 6), dim), (blocks,), jnp.float32, least / len(cuts), high / len(cuts))
        level = level * jnp.repeat(jnp.exp(heights), extent[dim] // blocks).reshape((-1,) + (1,) * (len(extent) - 1 - dim))
    return level


def shared_out(rng, own, number, rows, count, top, most, skew):
    order = jax.random.permutation(rng, count)
    packed, ordinary = load_shares(count, rows * top, most, skew, True), load_shares(count, rows * top, most, skew, False)
    places = jnp.arange(count)

    def named(lengths, offset_by):
        used = int((lengths > 0).sum())
        fixed = max(1, used // 4)
        moved = fixed + (places - fixed + offset_by * (used - fixed)) % max(1, count - fixed)
        return jnp.zeros((count,), jnp.int32).at[order[jnp.where(places < fixed, places, moved)]].set(jnp.asarray(lengths, jnp.int32))

    lengths = jnp.where(number % 4 == 0, named(packed, number // 4), named(ordinary, number - number // 4 - 1))
    mixed = jax.random.permutation(jax.random.fold_in(own, 3), count)
    donor, sink = mixed[0:count // 2 * 2:2], mixed[1:count // 2 * 2:2]
    room = jnp.minimum(lengths[donor] - 1, most - lengths[sink]) // 2
    room = jnp.where((donor == order[0]) | (sink == order[0]) | (lengths[sink] == 0), 0, jnp.maximum(room, 0))
    moved = jax.random.randint(jax.random.fold_in(own, 4), (count // 2,), 0, 1 << 20) % (room + 1)
    lengths = lengths.at[donor].add(-moved).at[sink].add(moved)
    items = jnp.searchsorted(jnp.cumsum(lengths), jnp.arange(rows * top), side="right").astype(jnp.int32)
    listing = items.reshape(top, rows).T
    listing = listing[jax.random.permutation(jax.random.fold_in(own, 1), rows)]
    offset_by = jax.random.randint(jax.random.fold_in(own, 2), (rows, 1), 0, top)
    return jnp.take_along_axis(listing, (jnp.arange(top)[None, :] + offset_by) % top, axis=1)


def load_shares(count, total, reach, lean, full):
    portions = [(1 << 20) // math.isqrt(grade ** lean) + 1 for grade in range(1, count + 1)]
    largest = reach if full else min(reach, max(-(-total // count), total * portions[0] // sum(portions)))
    least = 1 if total - largest >= count - 1 else 0
    given, spare = [largest] + [least] * (count - 1), total - largest - least * (count - 1)
    while spare > 0:
        movable = [i for i in range(1, count) if given[i] < largest] or [i for i in range(1, count) if given[i] < reach]
        mass, remaining = sum([portions[i] for i in movable]), spare
        for i in movable:
            extra = min(reach - given[i], max(1, remaining * portions[i] // mass), spare)
            given[i] = given[i] + extra
            spare = spare - extra
    return np.array(given)


def scatter_about(rng, shape, scale, limit, cuts=(), held_as=jnp.bfloat16):
    level = levels(rng, shape, cuts, -0.22, 0.18) if cuts else 1.0
    values = jax.random.normal(rng, shape, jnp.float32) * scale * level
    return jnp.minimum(jnp.maximum(values, -limit), limit).astype(held_as)


def setup_inputs(seed: int = 0) -> dict:
    key_of = jax.random.split(jax.random.key(seed), 8)
    states = scatter_about(key_of[0], (SECTIONS, TOKS, D), 1.0, 6.0, ((0, 32), (1, 32)))
    norm_gain = jnp.clip(1.0 + 0.18 * jax.random.normal(key_of[1], (SECTIONS, D), jnp.float32), 0.1, 1.9)
    router = scatter_about(key_of[2], (SECTIONS, D, EXPERTS), D ** -0.5, 0.09375, ((0, 32),))
    w_gate = scatter_about(key_of[3], (SECTIONS, D, EXPERTS * FF), D ** -0.5, 0.09375, ((0, 32), (2, 32)))
    w_up = scatter_about(key_of[4], (SECTIONS, D, EXPERTS * FF), D ** -0.5, 0.09375, ((0, 32), (2, 32)))
    w_down = scatter_about(key_of[5], (SECTIONS, EXPERTS * FF, D), FF ** -0.5, 0.1875, ((0, 32), (1, 32)))
    routes_keys = jax.random.split(jax.random.fold_in(key_of[6], 1), TICKS * SECTIONS * TOKS // TOK_DEV)
    routes_turns = jax.random.permutation(jax.random.fold_in(key_of[6], 3), TICKS * SECTIONS * TOKS // TOK_DEV)
    routes = jax.vmap(lambda own, number: shared_out(jax.random.fold_in(key_of[6], 2), own, number, TOK_DEV, EXPERTS, TOPK, CAP, 2))(routes_keys, routes_turns).reshape((TICKS, SECTIONS, TOKS, TOPK))
    return dict(states=states, norm_gain=norm_gain, router=router, w_gate=w_gate, w_up=w_up, w_down=w_down, routes=routes)


EPSILON = 1e-06

def normalize(states, gain):
    values = states.astype(jnp.float32)
    meansq = lax.optimization_barrier(jnp.mean(values * values, axis=-1, keepdims=True))
    return (values * lax.rsqrt(meansq + EPSILON) * gain).astype(jnp.bfloat16)

def slot_positions(expert_ids, experts, sources):
    onehot = (expert_ids[:, :, None] == jnp.arange(experts, dtype=jnp.int32)).astype(jnp.int32)
    named = lax.optimization_barrier(jnp.sum(onehot, axis=1))
    grouped = named.reshape(sources, -1, experts)
    before = (jnp.cumsum(grouped, axis=1) - grouped).reshape(-1, experts)
    position = lax.optimization_barrier(jnp.sum(onehot * before[:, None, :], axis=2))
    return (onehot, position)

def gate_values(normed, router, onehot):
    logits = jnp.dot(normed, router, preferred_element_type=jnp.float32)
    affinity = jax.nn.sigmoid(logits)
    chosen = lax.optimization_barrier(jnp.sum(onehot.astype(jnp.float32) * affinity[:, None, :], axis=2))
    return chosen / lax.optimization_barrier(jnp.sum(chosen, axis=1, keepdims=True))

def layer(states, gain, router, w_gate, w_up, w_down, expert_ids):
    normed = normalize(states, gain)
    onehot, position = slot_positions(expert_ids, EXPERTS, N_EXPERT)
    gates = gate_values(normed, router, onehot)
    source = (jnp.arange(TOKS, dtype=jnp.int32) // TOK_DEV)[:, None]
    column = source * CAP + position
    buffers = jnp.zeros((EXPERTS, N_EXPERT * CAP, D), jnp.bfloat16)
    spread_rows = jnp.broadcast_to(normed[:, None, :], (TOKS, TOPK, D))
    buffers = buffers.at[expert_ids, column].set(spread_rows)
    inputs = buffers.astype(jnp.float32)
    gate_matrix = w_gate.astype(jnp.float32).reshape(D, EXPERTS, FF)
    lift_matrix = w_up.astype(jnp.float32).reshape(D, EXPERTS, FF)
    gate_out = jnp.einsum('erd,def->erf', inputs, gate_matrix)
    lifted = jnp.einsum('erd,def->erf', inputs, lift_matrix)
    hidden = (jax.nn.silu(gate_out) * lifted).astype(jnp.bfloat16)
    pieces = hidden.astype(jnp.float32).reshape(EXPERTS, N_EXPERT * CAP, SHARDS, HID_DEV)
    down_matrix = w_down.astype(jnp.float32).reshape(EXPERTS, SHARDS, HID_DEV, D)
    partial_value = jnp.einsum('ersh,eshd->ersd', pieces, down_matrix).astype(jnp.bfloat16)
    partial_value = lax.optimization_barrier(partial_value)
    expert_out = lax.optimization_barrier(jnp.sum(partial_value.astype(jnp.float32), axis=2))
    picked = expert_out[expert_ids, column]
    mixed = lax.optimization_barrier(jnp.sum(picked * gates[:, :, None], axis=1))
    return (states.astype(jnp.float32) + mixed).astype(jnp.bfloat16)

def one_section(operands):
    return layer(*operands)

def reference(states, norm_gain, router, w_gate, w_up, w_down, routes):
    for tick_index in range(TICKS):
        updated = lax.map(one_section, (states, norm_gain, router, w_gate, w_up, w_down, routes[tick_index]))
        states = jnp.roll(updated, 1, axis=0)
    return states
```

```python
import jax
import jax.numpy as jnp
from jax import lax
from jax.sharding import PartitionSpec as P

TICKS = 2
EPSILON = 1e-06


def normalize(states, gain):
    values = states.astype(jnp.float32)
    meansq = jnp.mean(values * values, axis=-1, keepdims=True)
    return (values * lax.rsqrt(meansq + EPSILON) * gain).astype(jnp.bfloat16)


def dense_gates(normed, router, expert_ids):
    experts = router.shape[1]
    affinity = jax.nn.sigmoid(jnp.dot(normed, router, preferred_element_type=jnp.float32))
    named = jnp.any(expert_ids[:, :, None] == jnp.arange(experts, dtype=jnp.int32), axis=1)
    chosen = jnp.where(named, affinity, 0.0)
    return chosen / jnp.sum(chosen, axis=1, keepdims=True)


def on_device(states, norm_gain, router, w_gate, w_up, w_down, routes):
    devices = lax.axis_size("expert")
    experts = router.shape[2]
    shards = devices // experts
    width = states.shape[2]
    mine = lax.axis_index("expert") // shards
    current = states[0]
    sections = lax.axis_size("section")
    for tick in range(TICKS):
        normed = normalize(current, norm_gain[0])
        gates = dense_gates(normed, router[0], routes[tick, 0])
        high = gates.astype(jnp.bfloat16)
        low = (gates - high.astype(jnp.float32)).astype(jnp.bfloat16)
        block = jnp.concatenate(
            [normed, jnp.pad(jnp.concatenate([high, low], axis=1), ((0, 0), (0, 128 - 2 * experts)))],
            axis=1,
        )
        rows = lax.all_gather(block, "expert", axis=0, tiled=True)
        extra = rows[:, width:].astype(jnp.float32)
        picked = jnp.arange(128, dtype=jnp.int32) % experts == mine
        picked = picked & (jnp.arange(128, dtype=jnp.int32) < 2 * experts)
        gate = jnp.sum(jnp.where(picked, extra, 0.0), axis=1, keepdims=True)
        rows = rows[:, :width]
        gate_out = jnp.dot(rows, w_gate[0], preferred_element_type=jnp.float32)
        lifted = jnp.dot(rows, w_up[0], preferred_element_type=jnp.float32)
        hidden = (jax.nn.silu(gate_out) * lifted * gate).astype(jnp.bfloat16)
        partial = jnp.dot(hidden, w_down[0], preferred_element_type=jnp.float32).astype(jnp.bfloat16)
        mixed = lax.psum_scatter(partial, "expert", scatter_dimension=0, tiled=True)
        updated = (current.astype(jnp.float32) + mixed.astype(jnp.float32)).astype(jnp.bfloat16)
        current = lax.ppermute(updated, "section", [(s, (s + 1) % sections) for s in range(sections)])
    return current[None]


def solution(mesh):
    placed = (
        P("section", "expert", None),
        P("section", None),
        P("section", None, None),
        P("section", None, "expert"),
        P("section", None, "expert"),
        P("section", "expert", None),
        P(None, "section", "expert", None),
    )
    return jax.shard_map(
        on_device,
        mesh=mesh,
        in_specs=placed,
        out_specs=P("section", "expert", None),
        check_vma=False,
    )
```

```python
import jax
import jax.numpy as jnp
from jax import lax
from jax.experimental import pallas as pl
from jax.experimental.pallas import tpu as pltpu
from jax.sharding import PartitionSpec as P

TICKS = 2
EPSILON = 1e-06
RING = 4
LINE = 8
SKIP = 2
LANES = 128
MESH = pl.DeviceIdType.MESH


def kernel(
    x_ref, gain_ref, router_ref, routes_ref, gate_ref, lift_ref, down_ref, out_ref,
    state, rows, w_gate, w_lift, w_out, part, near, line_out, line_in, updated, acc,
    load_sem, gl, gs, gr, rs, rr, hop_s, hop_r,
):
    tok, width = x_ref.shape
    experts = router_ref.shape[0]
    hid = gate_ref.shape[1]
    wide = rows.shape[-1]
    me = lax.axis_index("expert")
    sect = lax.axis_index("section")
    sections = lax.axis_size("section")
    x, z = lax.rem(me, RING), lax.div(me, RING)
    nxt, prv = lax.rem(sect + 1, sections), lax.rem(sect + sections - 1, sections)
    mine = lax.div(me, LINE * RING // experts)

    loads = (
        pltpu.make_async_copy(gate_ref, w_gate, load_sem.at[0]),
        pltpu.make_async_copy(lift_ref, w_lift, load_sem.at[1]),
        pltpu.make_async_copy(down_ref, w_out, load_sem.at[2]),
    )
    for load in loads:
        load.start()

    barrier = pltpu.get_barrier_semaphore()
    for d in range(1, RING):
        other = z * RING + lax.rem(x + d, RING)
        pl.semaphore_signal(barrier, inc=1, device_id={"expert": other}, device_id_type=MESH)
    for d in range(1, LINE):
        other = lax.rem(z + d, LINE) * RING + x
        pl.semaphore_signal(barrier, inc=1, device_id={"expert": other}, device_id_type=MESH)
    for other in (nxt, prv):
        pl.semaphore_signal(barrier, inc=1, device_id={"section": other}, device_id_type=MESH)
    state[0] = x_ref[...]
    pl.semaphore_wait(barrier, RING - 1 + LINE - 1 + 2)

    def send(src, dst, ssem, rsem, device):
        return pltpu.make_async_remote_copy(
            src_ref=src, dst_ref=dst, send_sem=ssem, recv_sem=rsem, device_id=device, device_id_type=MESH
        )

    def inside(zb):
        return (zb >= 0) & (zb < LINE)

    def both_sides(k, work):
        for zb in (z - k, z + k):

            @pl.when(inside(zb))
            def _():
                work(zb)

    def tick(t, carry):
        def g_line(side, reach, owner):
            block = rows.at[t, owner, x]
            target = z + (reach if side == 0 else -reach)
            return send(
                block, block, gl.at[t, side * SKIP + reach - 1, owner], gr.at[t, 0, owner], {"expert": target * RING + x}
            )

        def relays(owner, act):
            for side in range(2):
                for reach in range(1, SKIP + 1):
                    away = z - owner if side == 0 else owner - z
                    target = z + (reach if side == 0 else -reach)

                    @pl.when((away >= 0) & (lax.rem(away + 8 * SKIP, SKIP) == 0) & inside(target))
                    def _():
                        act(g_line(side, reach, owner))

        def g_ring(d, zb, owner):
            block = rows.at[t, zb, owner]
            return send(block, block, gs.at[t, d, zb], gr.at[t, d, zb], {"expert": z * RING + lax.rem(x + d, RING)})

        values = state[t].astype(jnp.float32)
        meansq = jnp.mean(values * values, axis=-1, keepdims=True)
        normed = (values * lax.rsqrt(meansq + EPSILON) * gain_ref[...]).astype(jnp.bfloat16)
        rows[t, z, x, :, pl.ds(0, width)] = normed
        normed = normed.astype(jnp.float32)
        square = (tok, tok)
        same = lax.broadcasted_iota(jnp.int32, square, 0) == lax.broadcasted_iota(jnp.int32, square, 1)
        ids = [
            jnp.sum(jnp.where(same, jnp.broadcast_to(picks, square), 0.0), axis=1, keepdims=True)
            for picks in (routes_ref[t, k : k + 1, :].astype(jnp.float32) for k in range(routes_ref.shape[1]))
        ]
        chosen = []
        for e in range(experts):
            logit = jnp.sum(normed * router_ref[e : e + 1, :].astype(jnp.float32), axis=1, keepdims=True)
            named = sum(jnp.where(one == e, 1.0, 0.0) for one in ids)
            chosen.append(named * jax.nn.sigmoid(logit))
        total = sum(chosen[1:], chosen[0])
        lane = lax.broadcasted_iota(jnp.int32, (tok, LANES), 1)
        extra = jnp.zeros((tok, LANES), jnp.float32)
        for e in range(experts):
            gate = chosen[e] / total
            high = gate.astype(jnp.bfloat16).astype(jnp.float32)
            extra = jnp.where(lane == e, high, extra)
            extra = jnp.where(lane == experts + e, gate - high, extra)
        rows[t, z, x, :, pl.ds(width, LANES)] = extra.astype(jnp.bfloat16)

        def ring_sends(zb):
            for d in range(1, RING):
                g_ring(d, zb, x).start()

        def line_arrived(zb):
            g_line(0, 1, zb).wait_recv()
            relays(zb, lambda copy: copy.start())
            ring_sends(zb)

        def ring_arrived(zb, carry):
            for d in range(1, RING):
                g_ring(d, zb, lax.rem(x + RING - d, RING)).wait_recv()
            return carry

        def outward(first, work):
            def one(k, carry):
                both_sides(k, work)
                return carry

            lax.fori_loop(first, LINE, one, 0)

        relays(z, lambda copy: copy.start())
        ring_sends(z)
        outward(1, line_arrived)
        lax.fori_loop(0, LINE, ring_arrived, 0)

        @pl.when(t == 0)
        def _():
            for load in loads:
                load.wait()

        flat = rows[t].reshape(LINE * RING * tok, wide)
        lane = lax.broadcasted_iota(jnp.int32, (LINE * RING * tok, LANES), 1)
        extra = flat[:, width:].astype(jnp.float32)
        weight = jnp.sum(
            jnp.where((lane == mine) | (lane == mine + experts), extra, 0.0), axis=1, keepdims=True
        )
        w_in = jnp.concatenate([w_gate[...], w_lift[...]], axis=1)
        both = jnp.dot(flat[:, :width], w_in, preferred_element_type=jnp.float32)
        gate_out, lifted = both[:, :hid], both[:, hid:]
        hidden = (gate_out / (1.0 + jnp.exp(-gate_out)) * lifted * weight).astype(jnp.bfloat16)
        span = 512
        for c in range(width // span):
            cols = pl.ds(c * span, span)
            made = jnp.dot(hidden, w_out[:, cols], preferred_element_type=jnp.float32)
            part[t, :, :, :, cols] = made.astype(jnp.bfloat16).reshape(LINE, RING, tok, span)

        def r_ring(d, zb):
            other = lax.rem(x + d, RING)
            return send(
                part.at[t, zb, other], near.at[t, d - 1, zb], rs.at[t, d, zb], rr.at[t, d, zb], {"expert": z * RING + other}
            )

        def r_line(zb, owner):
            return send(
                line_out.at[t, zb], line_in.at[t, owner], rs.at[t, 0, zb], rr.at[t, 0, owner], {"expert": zb * RING + x}
            )

        def ring_reduce(zb):
            for d in range(1, RING):
                r_ring(d, zb).start()

        def ring_sum(zb):
            total = part[t, zb, x].astype(jnp.float32)
            for d in range(1, RING):
                r_ring(d, zb).wait_recv()
                total = total + near[t, d - 1, zb].astype(jnp.float32)
            return total

        def line_reduce(zb):
            line_out[t, zb] = ring_sum(zb).astype(jnp.bfloat16)
            r_line(zb, z).start()

        def line_sum(zb):
            r_line(z, zb).wait_recv()
            acc[...] += line_in[t, zb].astype(jnp.float32)

        def inward(work):
            def one(i, carry):
                both_sides(LINE - 1 - i, work)
                return carry

            lax.fori_loop(0, LINE - 1, one, 0)

        inward(ring_reduce)
        ring_reduce(z)
        inward(line_reduce)
        acc[...] = ring_sum(z) + state[t].astype(jnp.float32)
        inward(line_sum)
        updated[t] = acc[...].astype(jnp.bfloat16)
        hop = send(updated.at[t], state.at[t + 1], hop_s.at[t], hop_r.at[t], {"section": nxt})
        hop.start()

        def finish(zb, carry):
            for d in range(1, RING):
                g_ring(d, zb, x).wait_send()
                r_ring(d, zb).wait_send()

            @pl.when(zb != z)
            def _():
                r_line(zb, z).wait_send()

            relays(zb, lambda copy: copy.wait_send())
            return carry

        lax.fori_loop(0, LINE, finish, 0)
        hop.wait_recv()
        hop.wait_send()
        return carry

    lax.fori_loop(0, TICKS, tick, 0)
    out_ref[...] = state[TICKS]


def on_device(states, norm_gain, router, w_gate, w_up, w_down, routes):
    tok, width = states.shape[1:]
    hid = w_gate.shape[2]
    vmem, hbm = pl.BlockSpec(memory_space=pltpu.VMEM), pl.BlockSpec(memory_space=pl.ANY)
    half = jnp.bfloat16
    made = pl.pallas_call(
        kernel,
        out_shape=jax.ShapeDtypeStruct((tok, width), half),
        in_specs=[vmem, vmem, vmem, vmem, hbm, hbm, hbm],
        out_specs=vmem,
        scratch_shapes=[
            pltpu.VMEM((TICKS + 1, tok, width), half),
            pltpu.VMEM((TICKS, LINE, RING, tok, width + LANES), half),
            pltpu.VMEM((width, hid), half),
            pltpu.VMEM((width, hid), half),
            pltpu.VMEM((hid, width), half),
            pltpu.VMEM((TICKS, LINE, RING, tok, width), half),
            pltpu.VMEM((TICKS, RING - 1, LINE, tok, width), half),
            pltpu.VMEM((TICKS, LINE, tok, width), half),
            pltpu.VMEM((TICKS, LINE, tok, width), half),
            pltpu.VMEM((TICKS, tok, width), half),
            pltpu.VMEM((tok, width), jnp.float32),
            pltpu.SemaphoreType.DMA((3,)),
            pltpu.SemaphoreType.DMA((TICKS, 2 * SKIP, LINE)),
            pltpu.SemaphoreType.DMA((TICKS, RING, LINE)),
            pltpu.SemaphoreType.DMA((TICKS, RING, LINE)),
            pltpu.SemaphoreType.DMA((TICKS, RING, LINE)),
            pltpu.SemaphoreType.DMA((TICKS, RING, LINE)),
            pltpu.SemaphoreType.DMA((TICKS,)),
            pltpu.SemaphoreType.DMA((TICKS,)),
        ],
        compiler_params=pltpu.CompilerParams(
            collective_id=0, has_side_effects=True, vmem_limit_bytes=56 * 2**20
        ),
    )(
        states[0],
        norm_gain,
        jnp.transpose(router[0]),
        jnp.transpose(routes[:, 0], (0, 2, 1)),
        w_gate[0],
        w_up[0],
        w_down[0],
    )
    return made[None]


def solution(mesh):
    placed = (
        P("section", "expert", None),
        P("section", None),
        P("section", None, None),
        P("section", None, "expert"),
        P("section", None, "expert"),
        P("section", "expert", None),
        P(None, "section", "expert", None),
    )
    return jax.shard_map(
        on_device,
        mesh=mesh,
        in_specs=placed,
        out_specs=P("section", "expert", None),
        check_vma=False,
    )
```

```python
import jax
import jax.numpy as jnp
from jax import lax
from jax.experimental import pallas as pl
from jax.experimental.pallas import tpu as pltpu
from jax.sharding import PartitionSpec as P

TICKS = 2
EPSILON = 1e-06
RING = 4
LINE = 8
FIRST = 4
SKIP = 2
LANES = 128
MESH = pl.DeviceIdType.MESH


def kernel(
    x_ref, gain_ref, router_ref, routes_ref, gate_ref, lift_ref, down_ref, out_ref,
    state, rows, w_gate, w_lift, w_out, part, near, line_out, line_in, updated, acc,
    load_sem, frs, frr, fls, flr, gl, gs, gr, rs, rr, hop_s, hop_r,
):
    tok, width = x_ref.shape
    experts = router_ref.shape[0]
    hid = gate_ref.shape[1]
    wide = rows.shape[-1]
    first = FIRST * LANES
    me = lax.axis_index("expert")
    sect = lax.axis_index("section")
    sections = lax.axis_size("section")
    x, z = lax.rem(me, RING), lax.div(me, RING)
    nxt, prv = lax.rem(sect + 1, sections), lax.rem(sect + sections - 1, sections)
    mine = lax.div(me, LINE * RING // experts)

    loads = (
        pltpu.make_async_copy(gate_ref, w_gate, load_sem.at[0]),
        pltpu.make_async_copy(lift_ref, w_lift, load_sem.at[1]),
        pltpu.make_async_copy(down_ref, w_out, load_sem.at[2]),
    )
    for load in loads:
        load.start()

    barrier = pltpu.get_barrier_semaphore()
    for d in range(1, RING):
        other = z * RING + lax.rem(x + d, RING)
        pl.semaphore_signal(barrier, inc=1, device_id={"expert": other}, device_id_type=MESH)
    for d in range(1, LINE):
        other = lax.rem(z + d, LINE) * RING + x
        pl.semaphore_signal(barrier, inc=1, device_id={"expert": other}, device_id_type=MESH)
    for other in (nxt, prv):
        pl.semaphore_signal(barrier, inc=1, device_id={"section": other}, device_id_type=MESH)
    state[0] = x_ref[...]
    pl.semaphore_wait(barrier, RING - 1 + LINE - 1 + 2)

    def send(src, dst, ssem, rsem, device):
        return pltpu.make_async_remote_copy(
            src_ref=src, dst_ref=dst, send_sem=ssem, recv_sem=rsem, device_id=device, device_id_type=MESH
        )

    def inside(zb):
        return (zb >= 0) & (zb < LINE)

    def both_sides(k, work):
        for zb in (z - k, z + k):

            @pl.when(inside(zb))
            def _():
                work(zb)

    def tick(t, carry):
        def g_line(side, reach, owner):
            block = rows.at[t, owner, x, :, pl.ds(first, wide - first)]
            target = z + (reach if side == 0 else -reach)
            return send(
                block, block, gl.at[t, side * SKIP + reach - 1, owner], gr.at[t, 0, owner], {"expert": target * RING + x}
            )

        def relays(owner, act, make=g_line):
            for side in range(2):
                for reach in range(1, SKIP + 1):
                    away = z - owner if side == 0 else owner - z
                    target = z + (reach if side == 0 else -reach)

                    @pl.when((away >= 0) & (lax.rem(away + 8 * SKIP, SKIP) == 0) & inside(target))
                    def _():
                        act(make(side, reach, owner))

        def f_ring(d, owner):
            block = rows.at[t, z, owner, :, pl.ds(0, first)]
            device = {"expert": z * RING + lax.rem(x + d, RING)}
            return send(block, block, frs.at[t, d], frr.at[t, d], device)

        def f_line(column):
            def make(side, reach, owner):
                block = rows.at[t, owner, column, :, pl.ds(0, first)]
                target = z + (reach if side == 0 else -reach)
                slot = column * 2 * SKIP + side * SKIP + reach - 1
                device = {"expert": target * RING + x}
                return send(block, block, fls.at[t, slot, owner], flr.at[t, column, owner], device)

            return make

        def f_relays(owner, column, act):
            relays(owner, act, f_line(column))

        def f_arrived(zb):
            def one(column, carry):
                f_line(column)(0, 1, zb).wait_recv()
                f_relays(zb, column, lambda copy: copy.start())
                return carry

            lax.fori_loop(0, RING, one, 0)

        def g_ring(d, zb, owner):
            block = rows.at[t, zb, owner, :, pl.ds(first, wide - first)]
            return send(block, block, gs.at[t, d, zb], gr.at[t, d, zb], {"expert": z * RING + lax.rem(x + d, RING)})

        values = state[t].astype(jnp.float32)
        meansq = jnp.mean(values * values, axis=-1, keepdims=True)
        normed = (values * lax.rsqrt(meansq + EPSILON) * gain_ref[...]).astype(jnp.bfloat16)
        rows[t, z, x, :, pl.ds(0, width)] = normed
        normed = normed.astype(jnp.float32)
        square = (tok, tok)
        same = lax.broadcasted_iota(jnp.int32, square, 0) == lax.broadcasted_iota(jnp.int32, square, 1)
        ids = [
            jnp.sum(jnp.where(same, jnp.broadcast_to(picks, square), 0.0), axis=1, keepdims=True)
            for picks in (routes_ref[t, k : k + 1, :].astype(jnp.float32) for k in range(routes_ref.shape[1]))
        ]
        chosen = []
        for e in range(experts):
            logit = jnp.sum(normed * router_ref[e : e + 1, :].astype(jnp.float32), axis=1, keepdims=True)
            named = sum(jnp.where(one == e, 1.0, 0.0) for one in ids)
            chosen.append(named * jax.nn.sigmoid(logit))
        total = sum(chosen[1:], chosen[0])
        lane = lax.broadcasted_iota(jnp.int32, (tok, LANES), 1)
        extra = jnp.zeros((tok, LANES), jnp.float32)
        for e in range(experts):
            gate = chosen[e] / total
            high = gate.astype(jnp.bfloat16).astype(jnp.float32)
            extra = jnp.where(lane == e, high, extra)
            extra = jnp.where(lane == experts + e, gate - high, extra)
        rows[t, z, x, :, pl.ds(width, LANES)] = extra.astype(jnp.bfloat16)

        def ring_sends(zb):
            for d in range(1, RING):
                g_ring(d, zb, x).start()

        def line_arrived(zb):
            g_line(0, 1, zb).wait_recv()
            relays(zb, lambda copy: copy.start())
            ring_sends(zb)

        def ring_arrived(zb, carry):
            for d in range(1, RING):
                g_ring(d, zb, lax.rem(x + RING - d, RING)).wait_recv()
            return carry

        def outward(first, work):
            def one(k, carry):
                both_sides(k, work)
                return carry

            lax.fori_loop(first, LINE, one, 0)

        relays(z, lambda copy: copy.start())
        for d in (1, 3, 2):
            f_ring(d, x).start()
        f_relays(z, x, lambda copy: copy.start())
        ring_sends(z)
        for d in (1, 3, 2):
            f_ring(d, lax.rem(x + RING - d, RING)).wait_recv()
            f_relays(z, lax.rem(x + RING - d, RING), lambda copy: copy.start())

        def arrivals(k, carry):
            both_sides(k, line_arrived)

            @pl.when(k > 1)
            def _():
                both_sides(k - 1, f_arrived)

            return carry

        lax.fori_loop(1, LINE + 1, arrivals, 0)
        lax.fori_loop(0, LINE, ring_arrived, 0)

        @pl.when(t == 0)
        def _():
            for load in loads:
                load.wait()

        flat = rows[t].reshape(LINE * RING * tok, wide)
        lane = lax.broadcasted_iota(jnp.int32, (LINE * RING * tok, LANES), 1)
        extra = flat[:, width:].astype(jnp.float32)
        weight = jnp.sum(
            jnp.where((lane == mine) | (lane == mine + experts), extra, 0.0), axis=1, keepdims=True
        )
        w_in = jnp.concatenate([w_gate[...], w_lift[...]], axis=1)
        both = jnp.dot(flat[:, :width], w_in, preferred_element_type=jnp.float32)
        gate_out, lifted = both[:, :hid], both[:, hid:]
        hidden = (gate_out / (1.0 + jnp.exp(-gate_out)) * lifted * weight).astype(jnp.bfloat16)
        span = 512
        for c in range(width // span):
            cols = pl.ds(c * span, span)
            made = jnp.dot(hidden, w_out[:, cols], preferred_element_type=jnp.float32)
            part[t, :, :, :, cols] = made.astype(jnp.bfloat16).reshape(LINE, RING, tok, span)

        def r_ring(d, zb):
            other = lax.rem(x + d, RING)
            return send(
                part.at[t, zb, other], near.at[t, d - 1, zb], rs.at[t, d, zb], rr.at[t, d, zb], {"expert": z * RING + other}
            )

        def r_line(zb, owner):
            return send(
                line_out.at[t, zb], line_in.at[t, owner], rs.at[t, 0, zb], rr.at[t, 0, owner], {"expert": zb * RING + x}
            )

        def ring_reduce(zb):
            for d in range(1, RING):
                r_ring(d, zb).start()

        def ring_sum(zb):
            total = part[t, zb, x].astype(jnp.float32)
            for d in range(1, RING):
                r_ring(d, zb).wait_recv()
                total = total + near[t, d - 1, zb].astype(jnp.float32)
            return total

        def line_reduce(zb):
            line_out[t, zb] = ring_sum(zb).astype(jnp.bfloat16)
            r_line(zb, z).start()

        def line_sum(zb):
            r_line(z, zb).wait_recv()
            acc[...] += line_in[t, zb].astype(jnp.float32)

        def inward(work):
            def one(i, carry):
                both_sides(LINE - 1 - i, work)
                return carry

            lax.fori_loop(0, LINE - 1, one, 0)

        inward(ring_reduce)
        ring_reduce(z)

        def gathered(zb, carry):
            for d in range(1, RING):
                g_ring(d, zb, x).wait_send()

            relays(zb, lambda copy: copy.wait_send())

            def columns(column, carry):
                f_relays(zb, column, lambda copy: copy.wait_send())
                return carry

            lax.fori_loop(0, RING, columns, 0)
            return carry

        lax.fori_loop(0, LINE, gathered, 0)
        for d in range(1, RING):
            f_ring(d, x).wait_send()
        inward(line_reduce)
        acc[...] = ring_sum(z) + state[t].astype(jnp.float32)
        inward(line_sum)
        updated[t] = acc[...].astype(jnp.bfloat16)
        hop = send(updated.at[t], state.at[t + 1], hop_s.at[t], hop_r.at[t], {"section": nxt})
        hop.start()

        def finish(zb, carry):
            for d in range(1, RING):
                r_ring(d, zb).wait_send()

            @pl.when(zb != z)
            def _():
                r_line(zb, z).wait_send()

            return carry

        lax.fori_loop(0, LINE, finish, 0)
        hop.wait_recv()
        hop.wait_send()
        return carry

    lax.fori_loop(0, TICKS, tick, 0)
    out_ref[...] = state[TICKS]


def on_device(states, norm_gain, router, w_gate, w_up, w_down, routes):
    tok, width = states.shape[1:]
    hid = w_gate.shape[2]
    vmem, hbm = pl.BlockSpec(memory_space=pltpu.VMEM), pl.BlockSpec(memory_space=pl.ANY)
    half = jnp.bfloat16
    made = pl.pallas_call(
        kernel,
        out_shape=jax.ShapeDtypeStruct((tok, width), half),
        in_specs=[vmem, vmem, vmem, vmem, hbm, hbm, hbm],
        out_specs=vmem,
        scratch_shapes=[
            pltpu.VMEM((TICKS + 1, tok, width), half),
            pltpu.VMEM((TICKS, LINE, RING, tok, width + LANES), half),
            pltpu.VMEM((width, hid), half),
            pltpu.VMEM((width, hid), half),
            pltpu.VMEM((hid, width), half),
            pltpu.VMEM((TICKS, LINE, RING, tok, width), half),
            pltpu.VMEM((TICKS, RING - 1, LINE, tok, width), half),
            pltpu.VMEM((TICKS, LINE, tok, width), half),
            pltpu.VMEM((TICKS, LINE, tok, width), half),
            pltpu.VMEM((TICKS, tok, width), half),
            pltpu.VMEM((tok, width), jnp.float32),
            pltpu.SemaphoreType.DMA((3,)),
            pltpu.SemaphoreType.DMA((TICKS, RING)),
            pltpu.SemaphoreType.DMA((TICKS, RING)),
            pltpu.SemaphoreType.DMA((TICKS, RING * 2 * SKIP, LINE)),
            pltpu.SemaphoreType.DMA((TICKS, RING, LINE)),
            pltpu.SemaphoreType.DMA((TICKS, 2 * SKIP, LINE)),
            pltpu.SemaphoreType.DMA((TICKS, RING, LINE)),
            pltpu.SemaphoreType.DMA((TICKS, RING, LINE)),
            pltpu.SemaphoreType.DMA((TICKS, RING, LINE)),
            pltpu.SemaphoreType.DMA((TICKS, RING, LINE)),
            pltpu.SemaphoreType.DMA((TICKS,)),
            pltpu.SemaphoreType.DMA((TICKS,)),
        ],
        compiler_params=pltpu.CompilerParams(
            collective_id=0, has_side_effects=True, vmem_limit_bytes=56 * 2**20
        ),
    )(
        states[0],
        norm_gain,
        jnp.transpose(router[0]),
        jnp.transpose(routes[:, 0], (0, 2, 1)),
        w_gate[0],
        w_up[0],
        w_down[0],
    )
    return made[None]


def solution(mesh):
    placed = (
        P("section", "expert", None),
        P("section", None),
        P("section", None, None),
        P("section", None, "expert"),
        P("section", None, "expert"),
        P("section", "expert", None),
        P(None, "section", "expert", None),
    )
    return jax.shard_map(
        on_device,
        mesh=mesh,
        in_specs=placed,
        out_specs=P("section", "expert", None),
        check_vma=False,
    )
```

```python
import jax
import jax.numpy as jnp
from jax import lax
from jax.experimental import pallas as pl
from jax.experimental.pallas import tpu as pltpu
from jax.sharding import PartitionSpec as P

TICKS = 2
EPSILON = 1e-06
RING = 4
LINE = 8
FIRST = 4
SKIP = 2
LANES = 128
MESH = pl.DeviceIdType.MESH


def kernel(
    x_ref, gain_ref, router_ref, routes_ref, gate_ref, lift_ref, down_ref, out_ref,
    state, rows, w_gate, w_lift, w_out, part, near, line_out, line_in, updated, acc,
    load_sem, frs, frr, fls, flr, gl, gs, gr, rs, rr, hop_s, hop_r,
):
    tok, width = x_ref.shape
    experts = router_ref.shape[0]
    hid = gate_ref.shape[1]
    wide = rows.shape[-1]
    first = FIRST * LANES
    me = lax.axis_index("expert")
    sect = lax.axis_index("section")
    sections = lax.axis_size("section")
    x, z = lax.rem(me, RING), lax.div(me, RING)
    ring_next = {"expert": z * RING + lax.rem(x + 1, RING)}
    nxt, prv = lax.rem(sect + 1, sections), lax.rem(sect + sections - 1, sections)
    mine = lax.div(me, LINE * RING // experts)

    loads = (
        pltpu.make_async_copy(gate_ref, w_gate, load_sem.at[0]),
        pltpu.make_async_copy(lift_ref, w_lift, load_sem.at[1]),
        pltpu.make_async_copy(down_ref, w_out, load_sem.at[2]),
    )
    barrier = pltpu.get_barrier_semaphore()
    for d in range(1, RING):
        other = z * RING + lax.rem(x + d, RING)
        pl.semaphore_signal(barrier, inc=1, device_id={"expert": other}, device_id_type=MESH)
    for d in range(1, LINE):
        other = lax.rem(z + d, LINE) * RING + x
        pl.semaphore_signal(barrier, inc=1, device_id={"expert": other}, device_id_type=MESH)
    for other in (nxt, prv):
        pl.semaphore_signal(barrier, inc=1, device_id={"section": other}, device_id_type=MESH)
    for load in loads:
        load.start()
    state[0] = x_ref[...]
    pl.semaphore_wait(barrier, RING - 1 + LINE - 1 + 2)

    def send(src, dst, ssem, rsem, device):
        return pltpu.make_async_remote_copy(
            src_ref=src, dst_ref=dst, send_sem=ssem, recv_sem=rsem, device_id=device, device_id_type=MESH
        )

    def inside(zb):
        return (zb >= 0) & (zb < LINE)

    def both_sides(k, work):
        for zb in (z - k, z + k):

            @pl.when(inside(zb))
            def _():
                work(zb)

    def tick(t, carry):
        def g_line(side, reach, owner):
            block = rows.at[t, owner, x, :, pl.ds(first, wide - first)]
            target = z + (reach if side == 0 else -reach)
            return send(
                block, block, gl.at[t, side * SKIP + reach - 1, owner], gr.at[t, 0, owner], {"expert": target * RING + x}
            )

        def relays(owner, act, make=g_line):
            for side in range(2):
                for reach in range(1, SKIP + 1):
                    away = z - owner if side == 0 else owner - z
                    target = z + (reach if side == 0 else -reach)

                    @pl.when((away >= 0) & (lax.rem(away + 8 * SKIP, SKIP) == 0) & inside(target))
                    def _():
                        act(make(side, reach, owner))

        def f_ring(d, owner):
            block = rows.at[t, z, owner, :, pl.ds(0, first)]
            device = {"expert": z * RING + lax.rem(x + d, RING)}
            return send(block, block, frs.at[t, d], frr.at[t, d], device)

        def f_line(column):
            def make(side, reach, owner):
                block = rows.at[t, owner, column, :, pl.ds(0, first)]
                target = z + (reach if side == 0 else -reach)
                slot = column * 2 * SKIP + side * SKIP + reach - 1
                device = {"expert": target * RING + x}
                return send(block, block, fls.at[t, slot, owner], flr.at[t, column, owner], device)

            return make

        def f_relays(owner, column, act):
            relays(owner, act, f_line(column))

        def f_arrived(zb):
            def one(column, carry):
                block = rows.at[t, zb, column, :, pl.ds(0, first)]
                send(block, block, fls.at[t, 0, zb], flr.at[t, column, zb], ring_next).wait_recv()
                f_relays(zb, column, lambda copy: copy.start())
                return carry

            lax.fori_loop(0, RING, one, 0)

        def g_ring(d, zb, owner):
            block = rows.at[t, zb, owner, :, pl.ds(first, wide - first)]
            return send(block, block, gs.at[t, d, zb], gr.at[t, d, zb], {"expert": z * RING + lax.rem(x + d, RING)})

        values = state[t].astype(jnp.float32)
        meansq = jnp.mean(values * values, axis=-1, keepdims=True)
        normed = (values * lax.rsqrt(meansq + EPSILON) * gain_ref[...]).astype(jnp.bfloat16)
        rows[t, z, x, :, pl.ds(0, width)] = normed
        normed = normed.astype(jnp.float32)
        square = (tok, tok)
        same = lax.broadcasted_iota(jnp.int32, square, 0) == lax.broadcasted_iota(jnp.int32, square, 1)
        ids = [
            jnp.sum(jnp.where(same, jnp.broadcast_to(picks, square), 0.0), axis=1, keepdims=True)
            for picks in (routes_ref[t, k : k + 1, :].astype(jnp.float32) for k in range(routes_ref.shape[1]))
        ]
        chosen = []
        for e in range(experts):
            logit = jnp.sum(normed * router_ref[e : e + 1, :].astype(jnp.float32), axis=1, keepdims=True)
            named = sum(jnp.where(one == e, 1.0, 0.0) for one in ids)
            chosen.append(named * jax.nn.sigmoid(logit))
        total = sum(chosen[1:], chosen[0])
        lane = lax.broadcasted_iota(jnp.int32, (tok, LANES), 1)
        extra = jnp.zeros((tok, LANES), jnp.float32)
        for e in range(experts):
            gate = chosen[e] / total
            high = gate.astype(jnp.bfloat16).astype(jnp.float32)
            extra = jnp.where(lane == e, high, extra)
            extra = jnp.where(lane == experts + e, gate - high, extra)
        rows[t, z, x, :, pl.ds(width, LANES)] = extra.astype(jnp.bfloat16)

        def ring_sends(zb):
            for d in range(1, RING):
                g_ring(d, zb, x).start()

        def line_arrived(zb):
            block = rows.at[t, zb, x, :, pl.ds(first, wide - first)]
            send(block, block, gl.at[t, 0, zb], gr.at[t, 0, zb], ring_next).wait_recv()
            relays(zb, lambda copy: copy.start())
            ring_sends(zb)

        def ring_arrived(zb, carry):
            for d in range(1, RING):
                g_ring(d, zb, lax.rem(x + RING - d, RING)).wait_recv()
            return carry

        def outward(first, work):
            def one(k, carry):
                both_sides(k, work)
                return carry

            lax.fori_loop(first, LINE, one, 0)

        relays(z, lambda copy: copy.start())
        for d in (1, 3, 2):
            f_ring(d, x).start()
        f_relays(z, x, lambda copy: copy.start())
        ring_sends(z)
        for d in (1, 3, 2):
            f_ring(d, lax.rem(x + RING - d, RING)).wait_recv()
            f_relays(z, lax.rem(x + RING - d, RING), lambda copy: copy.start())

        def arrivals(k, carry):
            both_sides(k, line_arrived)

            @pl.when(k > 1)
            def _():
                both_sides(k - 1, f_arrived)

            return carry

        lax.fori_loop(1, LINE + 1, arrivals, 0)
        lax.fori_loop(0, LINE, ring_arrived, 0)

        @pl.when(t == 0)
        def _():
            for load in loads:
                load.wait()

        flat = rows[t].reshape(LINE * RING * tok, wide)
        lane = lax.broadcasted_iota(jnp.int32, (LINE * RING * tok, LANES), 1)
        extra = flat[:, width:].astype(jnp.float32)
        weight = jnp.sum(
            jnp.where((lane == mine) | (lane == mine + experts), extra, 0.0), axis=1, keepdims=True
        )
        w_in = jnp.concatenate([w_gate[...], w_lift[...]], axis=1)
        both = jnp.dot(flat[:, :width], w_in, preferred_element_type=jnp.float32)
        gate_out, lifted = both[:, :hid], both[:, hid:]
        hidden = (gate_out / (1.0 + jnp.exp(-gate_out)) * lifted * weight).astype(jnp.bfloat16)
        span = 512
        for c in range(width // span):
            cols = pl.ds(c * span, span)
            made = jnp.dot(hidden, w_out[:, cols], preferred_element_type=jnp.float32)
            part[t, :, :, :, cols] = made.astype(jnp.bfloat16).reshape(LINE, RING, tok, span)

        def r_ring(d, zb):
            other = lax.rem(x + d, RING)
            return send(
                part.at[t, zb, other], near.at[t, d - 1, zb], rs.at[t, d, zb], rr.at[t, d, zb], {"expert": z * RING + other}
            )

        def r_line(zb, owner):
            return send(
                line_out.at[t, zb], line_in.at[t, owner], rs.at[t, 0, zb], rr.at[t, 0, owner], {"expert": zb * RING + x}
            )

        def ring_reduce(zb):
            for d in range(1, RING):
                r_ring(d, zb).start()

        def ring_sum(zb):
            total = part[t, zb, x].astype(jnp.float32)
            for d in range(1, RING):
                r_ring(d, zb).wait_recv()
                total = total + near[t, d - 1, zb].astype(jnp.float32)
            return total

        def line_reduce(zb):
            line_out[t, zb] = ring_sum(zb).astype(jnp.bfloat16)
            r_line(zb, z).start()

        def line_sum(zb):
            r_line(z, zb).wait_recv()
            acc[...] += line_in[t, zb].astype(jnp.float32)

        def inward(work):
            def one(i, carry):
                both_sides(LINE - 1 - i, work)
                return carry

            lax.fori_loop(0, LINE - 1, one, 0)

        inward(ring_reduce)
        ring_reduce(z)

        def gathered(zb, carry):
            for d in range(1, RING):
                g_ring(d, zb, x).wait_send()

            relays(zb, lambda copy: copy.wait_send())

            def columns(column, carry):
                f_relays(zb, column, lambda copy: copy.wait_send())
                return carry

            lax.fori_loop(0, RING, columns, 0)
            return carry

        lax.fori_loop(0, LINE, gathered, 0)
        for d in range(1, RING):
            f_ring(d, x).wait_send()
        inward(line_reduce)
        acc[...] = ring_sum(z) + state[t].astype(jnp.float32)
        inward(line_sum)
        updated[t] = acc[...].astype(jnp.bfloat16)
        hop = send(updated.at[t], state.at[t + 1], hop_s.at[t], hop_r.at[t], {"section": nxt})
        hop.start()

        def finish(zb, carry):
            for d in range(1, RING):
                r_ring(d, zb).wait_send()

            @pl.when(zb != z)
            def _():
                r_line(zb, z).wait_send()

            return carry

        lax.fori_loop(0, LINE, finish, 0)
        hop.wait_recv()
        hop.wait_send()
        return carry

    lax.fori_loop(0, TICKS, tick, 0)
    out_ref[...] = state[TICKS]


def on_device(states, norm_gain, router, w_gate, w_up, w_down, routes):
    tok, width = states.shape[1:]
    hid = w_gate.shape[2]
    vmem, hbm = pl.BlockSpec(memory_space=pltpu.VMEM), pl.BlockSpec(memory_space=pl.ANY)
    half = jnp.bfloat16
    made = pl.pallas_call(
        kernel,
        out_shape=jax.ShapeDtypeStruct((tok, width), half),
        in_specs=[vmem, vmem, vmem, vmem, hbm, hbm, hbm],
        out_specs=vmem,
        scratch_shapes=[
            pltpu.VMEM((TICKS + 1, tok, width), half),
            pltpu.VMEM((TICKS, LINE, RING, tok, width + LANES), half),
            pltpu.VMEM((width, hid), half),
            pltpu.VMEM((width, hid), half),
            pltpu.VMEM((hid, width), half),
            pltpu.VMEM((TICKS, LINE, RING, tok, width), half),
            pltpu.VMEM((TICKS, RING - 1, LINE, tok, width), half),
            pltpu.VMEM((TICKS, LINE, tok, width), half),
            pltpu.VMEM((TICKS, LINE, tok, width), half),
            pltpu.VMEM((TICKS, tok, width), half),
            pltpu.VMEM((tok, width), jnp.float32),
            pltpu.SemaphoreType.DMA((3,)),
            pltpu.SemaphoreType.DMA((TICKS, RING)),
            pltpu.SemaphoreType.DMA((TICKS, RING)),
            pltpu.SemaphoreType.DMA((TICKS, RING * 2 * SKIP, LINE)),
            pltpu.SemaphoreType.DMA((TICKS, RING, LINE)),
            pltpu.SemaphoreType.DMA((TICKS, 2 * SKIP, LINE)),
            pltpu.SemaphoreType.DMA((TICKS, RING, LINE)),
            pltpu.SemaphoreType.DMA((TICKS, RING, LINE)),
            pltpu.SemaphoreType.DMA((TICKS, RING, LINE)),
            pltpu.SemaphoreType.DMA((TICKS, RING, LINE)),
            pltpu.SemaphoreType.DMA((TICKS,)),
            pltpu.SemaphoreType.DMA((TICKS,)),
        ],
        compiler_params=pltpu.CompilerParams(
            collective_id=0, has_side_effects=True, vmem_limit_bytes=56 * 2**20
        ),
    )(
        states[0],
        norm_gain,
        jnp.transpose(router[0]),
        jnp.transpose(routes[:, 0], (0, 2, 1)),
        w_gate[0],
        w_up[0],
        w_down[0],
    )
    return made[None]


def solution(mesh):
    placed = (
        P("section", "expert", None),
        P("section", None),
        P("section", None, None),
        P("section", None, "expert"),
        P("section", None, "expert"),
        P("section", "expert", None),
        P(None, "section", "expert", None),
    )
    return jax.shard_map(
        on_device,
        mesh=mesh,
        in_specs=placed,
        out_specs=P("section", "expert", None),
        check_vma=False,
    )
```
